256 devices in a mesh: blk: 16 (over y, z_lo), grp: 16 (over z_hi, x, core).
Axes of the slice: x: 4, y: 4, z: 8 (z_hi: 2, z_lo: 4; z = z_hi * 4 + z_lo), core: 2. Of those that a mesh axis runs over, the one named last changes fastest.
Arguments:
- images: bfloat16 [32768, 1152], P(('blk', 'grp')), may hold values from -0.1875 to 0.1875
- text_embed: bfloat16 [32768, 1152], P(('blk', 'grp')), may hold values from -0.1875 to 0.1875
- log_scale: float32 [1], replicated, may hold values from 3 to 4
- logit_bias: float32 [1], replicated, may hold values from -6 to -3
Outputs:
- image_grad: float32 [32768, 1152], P(('blk', 'grp'))
- text_grad: float32 [32768, 1152], P(('blk', 'grp'))
The draws below stay inside these ranges and needn't reach their ends.
All inputs are finite; a program needn't handle non-finite values.
Results may differ from the reference program's by a relative error of at most 0.0063.
Values may be sent and summed in bfloat16 or wider, within the bound.
A program may use at most 128 MiB of HBM per device.

```python
import jax
import jax.numpy as jnp
from jax import lax

D = 1152
ROWS = 128
STEPS = 2
BATCH = 32768
N_BLK = 16
N_GRP = 16


def shard_levels(own_key, dims, split, low, largest):
    def one(axis_at, shards_of):
        draws = jax.random.uniform(jax.random.fold_in(jax.random.fold_in(own_key, 6), axis_at), (shards_of,), jnp.float32, low / len(split), largest / len(split))
        return jnp.repeat(jnp.exp(draws), dims[axis_at] // shards_of).reshape((-1,) + (1,) * (len(dims) - axis_at - 1))

    level = one(*split[0])
    for cut in split[1:]:
        level = level * one(*cut)
    return level


def bell_draw(rng, shape, width, reach, pieces=(), kind=jnp.bfloat16):
    values = width * jax.random.normal(rng, shape, jnp.float32)
    if pieces:
        values = values * shard_levels(rng, shape, pieces, -0.22, 0.18)
    return jnp.clip(values, -reach, reach).astype(kind)


def setup_inputs(seed: int = 0) -> dict:
    arg_keys = jax.random.split(jax.random.key(seed), 5)
    images = bell_draw(arg_keys[0], (BATCH, D), 0.0295, 0.1875, ((0, 256),))
    text_embed = bell_draw(arg_keys[1], (BATCH, D), 0.0295, 0.1875, ((0, 256),))
    log_scale = jnp.clip(jax.random.uniform(arg_keys[2], (1,), jnp.float32, 3.0, 4.0), 3.0, 4.0)
    logit_bias = jnp.clip(jax.random.uniform(arg_keys[3], (1,), jnp.float32, -6.0, -3.0), -6.0, -3.0)
    return dict(images=images, text_embed=text_embed, log_scale=log_scale, logit_bias=logit_bias)


EPS = 1e-06

def unitize(embed):
    values = embed.astype(jnp.float32)
    inverse = lax.rsqrt(lax.optimization_barrier(jnp.sum(values * values, axis=-1, keepdims=True)) + EPS)
    return (values * inverse, inverse)

def reference(images, text_embed, log_scale, logit_bias):
    temper = jnp.exp(log_scale[0])
    offset = logit_bias[0]
    img_unit, img_inverse = unitize(images)
    txt_unit, txt_inverse = unitize(text_embed)
    group_rows = ROWS * N_GRP
    img_flat = img_unit.astype(jnp.bfloat16).reshape(N_BLK, group_rows, D).astype(jnp.float32)
    txt_flat = txt_unit.astype(jnp.bfloat16).reshape(N_BLK, group_rows, D).astype(jnp.float32)
    index_col = jnp.arange(group_rows, dtype=jnp.int32)
    identity = (index_col[:, None] == index_col[None, :]).astype(jnp.float32)
    img_grad = jnp.zeros((N_BLK, group_rows, D), jnp.float32)
    txt_grad = jnp.zeros((N_BLK, group_rows, D), jnp.float32)
    for section_index in range(STEPS):
        partner = jnp.roll(txt_flat, section_index, axis=0)
        logits = temper * jnp.einsum('gid,gjd->gij', img_flat, partner) + offset
        if section_index == 0:
            target = identity
        else:
            target = jnp.zeros_like(identity)
        pair_rounded = (temper * (jax.nn.sigmoid(logits) - target)).astype(jnp.bfloat16)
        pair_w = lax.optimization_barrier(pair_rounded).astype(jnp.float32)
        img_grad = img_grad + jnp.einsum('gij,gjd->gid', pair_w, partner)
        partial_sum = jnp.einsum('gij,gid->gjd', pair_w, img_flat)
        txt_grad = txt_grad + jnp.roll(partial_sum, -section_index, axis=0)
    img_grad = img_grad.reshape(N_BLK * group_rows, D)
    txt_grad = txt_grad.reshape(N_BLK * group_rows, D)
    image_out = img_inverse * (img_grad - lax.optimization_barrier(jnp.sum(img_grad * img_unit, axis=-1, keepdims=True)) * img_unit)
    text_out = txt_inverse * (txt_grad - lax.optimization_barrier(jnp.sum(txt_grad * txt_unit, axis=-1, keepdims=True)) * txt_unit)
    return (image_out, text_out)
```

```python
import functools

import jax
import jax.numpy as jnp
from jax import lax
from jax.experimental import pallas as pl
from jax.experimental.pallas import tpu as pltpu
from jax.sharding import PartitionSpec as P

EPS = 1e-06
R = 128
NX, NY, NZ = 4, 4, 8

SLOT = {2: 0, 1: 1, 3: 2, 0: 3}
FB = 80
RA = 48
FA = R - FB
OWN, P1 = 0, R
P2B, QA = 2 * R, 2 * R + FB
P2A, QB = 3 * R, 3 * R + FA


def kernel(
    img_hbm, txt_hbm, ls_ref, lb_ref, oimg_ref, otxt_ref,
    raw_img, raw_txt, imgs, txts, w_ref, wt_ref, dt_f, dt_b, back_in, own_in, far_in,
    di_f, di_out, di_in, xs, xh_in, xf_in, in_sem, send_sem, recv_sem,
):
    blk = lax.axis_index("blk")
    grp = lax.axis_index("grp")
    core = lax.rem(grp, 2)
    x = lax.rem(grp // 2, NX)
    z = lax.rem(blk, 4) + 4 * (grp // 8)

    def at(dblk, dz, dx=0, dcore=0):
        new_z = lax.rem(z + dz, NZ)
        new_x = lax.rem(x + dx, NX)
        new_core = lax.rem(core + dcore, 2)
        return (lax.rem(blk + dblk, 16), (new_z // 4 * NX + new_x) * 2 + new_core)

    near, near_back = at(1, 1), at(15, 7)
    far, far_back = at(1, 5), at(15, 3)
    right, left, twin = at(0, 0, 1), at(0, 0, 3), at(0, 0, 0, 1)

    load_txt = pltpu.make_async_copy(txt_hbm, raw_txt, in_sem.at[0])
    load_img = pltpu.make_async_copy(img_hbm, raw_img, in_sem.at[1])
    load_txt.start()
    load_img.start()
    barrier = pltpu.get_barrier_semaphore()
    peers = (near, near_back, far, far_back, right, left, twin)
    for peer in peers:
        pl.semaphore_signal(barrier, inc=1, device_id=peer, device_id_type=pl.DeviceIdType.MESH)

    copies = {}

    def send(name, src, dst, to):
        k = len(copies)
        copies[name] = pltpu.make_async_remote_copy(
            src_ref=src, dst_ref=dst, send_sem=send_sem.at[k], recv_sem=recv_sem.at[k],
            device_id=to, device_id_type=pl.DeviceIdType.MESH,
        )
        copies[name].start()

    def arrived(*names):
        for name in names:
            copies[name].wait_recv()

    def rows(ref, start, count):
        return ref.at[pl.ds(start, count)]

    def inverse_norm(raw):
        values = raw[...].astype(jnp.float32)
        return values, lax.rsqrt(jnp.sum(values * values, axis=-1, keepdims=True) + EPS)

    load_txt.wait()
    values, inverse = inverse_norm(raw_txt)
    txts[OWN:R, :] = (values * inverse).astype(jnp.bfloat16)
    pl.semaphore_wait(barrier, len(peers))

    send("n_a", rows(txts, FB, FA), rows(txts, P1 + FB, FA), near)
    send("f_b", rows(txts, 0, FB), rows(txts, P2B, FB), far)
    send("n_b", rows(txts, 0, FB), rows(txts, P1, FB), near)

    load_img.wait()
    values, inverse = inverse_norm(raw_img)
    imgs[7 * R : 8 * R, :] = (values * inverse).astype(jnp.bfloat16)

    def mine(dx):
        return (4 + SLOT[dx]) * R

    def other(dx):
        return SLOT[dx] * R

    half = R // 2
    send("r_lo", rows(imgs, mine(0), half), rows(imgs, mine(3), half), right)
    send("l_hi", rows(imgs, mine(0) + half, half), rows(imgs, mine(1) + half, half), left)
    send("r_hi", rows(imgs, mine(0) + half, half), rows(imgs, mine(3) + half, half), right)
    send("l_lo", rows(imgs, mine(0), half), rows(imgs, mine(1), half), left)
    send("t_0", rows(imgs, mine(0), R), rows(imgs, other(0), R), twin)

    arrived("n_a")
    send("o_a", rows(txts, P1 + FB, FA), rows(txts, QA, FA), far_back)
    arrived("r_lo")
    send("r2", rows(imgs, mine(3), half), rows(imgs, mine(2), half), right)
    arrived("l_hi")
    send("l2", rows(imgs, mine(1) + half, half), rows(imgs, mine(2) + half, half), left)
    arrived("r_hi")
    send("t_3", rows(imgs, mine(3), R), rows(imgs, other(3), R), twin)
    arrived("l_lo")
    send("t_1", rows(imgs, mine(1), R), rows(imgs, other(1), R), twin)
    arrived("f_b")
    send("o_b", rows(txts, P2B, FB), rows(txts, QB, FB), near_back)
    arrived("r2", "l2")
    send("t_2", rows(imgs, mine(2), R), rows(imgs, other(2), R), twin)
    arrived("o_a")
    send("f_a", rows(txts, QA, FA), rows(txts, P2A, FA), near)

    temper = jnp.exp(jnp.full((1, 256), ls_ref[0], jnp.float32))
    offset = jnp.full((1, 256), lb_ref[0], jnp.float32)

    def score(start, count, with_label):
        def tile(j, carry):
            cols = pl.ds(pl.multiple_of(j * 256, 256), 256)
            logits = lax.dot_general(
                txts[start : start + count, :], imgs[cols, :], (((1,), (1,)), ((), ())),
                preferred_element_type=jnp.float32,
            )
            weight = jax.nn.sigmoid(temper * logits + offset)
            if with_label:
                row = lax.broadcasted_iota(jnp.int32, (count, 256), 0) + (start + 7 * R)
                col = lax.broadcasted_iota(jnp.int32, (count, 256), 1) + j * 256
                weight = weight - (row == col).astype(jnp.float32)
            weight = (temper * weight).astype(jnp.bfloat16)
            w_ref[start : start + count, cols] = weight
            wt_ref[cols, start : start + count] = weight.T
            return carry

        lax.fori_loop(0, 4, tile, 0)

        def columns(cols):
            grad = jnp.dot(
                w_ref[start : start + count, :], imgs[:, cols], preferred_element_type=jnp.float32
            )
            dt_f[start : start + count, cols] = grad
            dt_b[start : start + count, cols] = grad.astype(jnp.bfloat16)

        def column_tile(j, carry):
            columns(pl.ds(pl.multiple_of(j * 256, 256), 256))
            return carry

        lax.fori_loop(0, 4, column_tile, 0)
        columns(pl.ds(1024, 128))

    def image_grads(pair, store):
        def columns(cols):
            store(cols, jnp.dot(
                wt_ref[pair * 256 : pair * 256 + 256, :], txts[:, cols],
                preferred_element_type=jnp.float32,
            ))

        def column_tile(j, carry):
            columns(pl.ds(pl.multiple_of(j * 256, 256), 256))
            return carry

        lax.fori_loop(0, 4, column_tile, 0)
        columns(pl.ds(1024, 128))

    def join(start, count, received):
        dt_b[start : start + count, :] = (
            dt_f[start : start + count, :] + received.astype(jnp.float32)
        ).astype(jnp.bfloat16)

    arrived("t_0", "t_3", "t_1", "t_2", "n_b")
    score(OWN, 2 * R, True)
    send("b_n", rows(dt_b, P1 + RA, R - RA), rows(own_in, RA, R - RA), near_back)

    score(P2B, R, False)
    send("b_fo", rows(dt_b, P2B, RA), rows(back_in, 0, RA), near_back)
    send("b_of_a", rows(dt_b, QA, FA), rows(back_in, 2 * RA + FB - RA, FA), near)

    arrived("o_b", "f_a")
    score(P2A, R, False)
    send("b_of_c", rows(dt_b, QB + RA, FB - RA), rows(back_in, 2 * RA, FB - RA), near)
    arrived("b_fo")
    join(QB, RA, back_in[0:RA, :])
    send("b_on", rows(dt_b, QB, RA), rows(back_in, RA, RA), far)
    arrived("b_of_a")
    join(P2A, FA, back_in[2 * RA + FB - RA : 2 * RA + R - RA, :])
    send("b_f_a", rows(dt_b, P2A, FA), rows(far_in, FB - RA, FA), far_back)

    def store_out(base):
        def store(cols, grad):
            di_out[base : base + 256, cols] = grad.astype(jnp.bfloat16)
        return store

    def store_keep(base):
        def store(cols, grad):
            di_f[base : base + 256, cols] = grad
        return store

    image_grads(0, store_out(0))
    send("c_2", rows(di_out, 0, R), rows(di_in, 0, R), twin)
    send("c_1", rows(di_out, R, R), rows(di_in, R, R), twin)
    arrived("b_of_c")
    join(P2B + RA, FB - RA, back_in[2 * RA : 2 * RA + FB - RA, :])
    send("b_f_c", rows(dt_b, P2B + RA, FB - RA), rows(far_in, 0, FB - RA), far_back)
    image_grads(1, store_out(2 * R))
    send("c_3", rows(di_out, 2 * R, R), rows(di_in, 2 * R, R), twin)
    send("c_0", rows(di_out, 3 * R, R), rows(di_in, 3 * R, R), twin)
    image_grads(2, store_keep(0))

    def both(start, count):
        return di_f[start : start + count, :] + di_in[start : start + count, :].astype(jnp.float32)

    arrived("c_2")
    xs[0:R, :] = both(0, R).astype(jnp.bfloat16)
    send("x2_r", rows(xs, 0, half), rows(xh_in, 0, half), right)
    send("x2_l", rows(xs, half, half), rows(xh_in, half, half), left)
    arrived("c_1")
    xs[R + half : 2 * R, :] = both(R + half, half).astype(jnp.bfloat16)
    send("x1_hi", rows(xs, R + half, half), rows(xf_in, half, half), right)
    image_grads(3, store_keep(2 * R))
    arrived("c_3")
    xs[2 * R : 2 * R + half, :] = both(2 * R, half).astype(jnp.bfloat16)
    send("x3_lo", rows(xs, 2 * R, half), rows(xf_in, R, half), left)
    arrived("x2_r")
    xs[R : R + half, :] = (both(R, half) + xh_in[0:half, :].astype(jnp.float32)).astype(jnp.bfloat16)
    send("x1_lo", rows(xs, R, half), rows(xf_in, 0, half), right)
    arrived("x2_l")
    xs[2 * R + half : 3 * R, :] = (
        both(2 * R + half, half) + xh_in[half:R, :].astype(jnp.float32)
    ).astype(jnp.bfloat16)
    send("x3_hi", rows(xs, 2 * R + half, half), rows(xf_in, R + half, half), left)

    arrived("b_on")
    join(P1, RA, back_in[RA : 2 * RA, :])
    send("b_n_a", rows(dt_b, P1, RA), rows(own_in, 0, RA), near_back)

    def project(raw, grad_hat):
        values, inverse = inverse_norm(raw)
        unit = values * inverse
        inner = jnp.sum(grad_hat * unit, axis=-1, keepdims=True)
        return inverse * (grad_hat - inner * unit)

    arrived("c_0", "x1_hi", "x3_lo", "x1_lo", "x3_hi")
    grad = both(3 * R, R) + xf_in[0:R, :].astype(jnp.float32) + xf_in[R : 2 * R, :].astype(jnp.float32)
    oimg_ref[...] = project(raw_img, grad)

    arrived("b_n", "b_f_a", "b_f_c", "b_n_a")
    dt_f[RA:R, :] = dt_f[RA:R, :] + far_in[...].astype(jnp.float32)
    otxt_ref[...] = project(raw_txt, dt_f[0:R, :] + own_in[...].astype(jnp.float32))
    for copy in copies.values():
        copy.wait_send()


def per_device(images, text_embed, log_scale, logit_bias):
    d = images.shape[1]
    bf, f32 = jnp.bfloat16, jnp.float32
    vmem, smem, hbm = (pl.BlockSpec(memory_space=m) for m in (pltpu.VMEM, pltpu.SMEM, pl.ANY))
    n_copies = 40
    return pl.pallas_call(
        kernel,
        out_shape=(jax.ShapeDtypeStruct((R, d), f32),) * 2,
        in_specs=[hbm, hbm, smem, smem],
        out_specs=(vmem, vmem),
        scratch_shapes=[
            pltpu.VMEM((R, d), bf),
            pltpu.VMEM((R, d), bf),
            pltpu.VMEM((8 * R, d), bf),
            pltpu.VMEM((4 * R, d), bf),
            pltpu.VMEM((4 * R, 8 * R), bf),
            pltpu.VMEM((8 * R, 4 * R), bf),
            pltpu.VMEM((4 * R, d), f32),
            pltpu.VMEM((4 * R, d), bf),
            pltpu.VMEM((R + RA, d), bf),
            pltpu.VMEM((R, d), bf),
            pltpu.VMEM((R - RA, d), bf),
            pltpu.VMEM((4 * R, d), f32),
            pltpu.VMEM((4 * R, d), bf),
            pltpu.VMEM((4 * R, d), bf),
            pltpu.VMEM((3 * R, d), bf),
            pltpu.VMEM((R, d), bf),
            pltpu.VMEM((2 * R, d), bf),
            pltpu.SemaphoreType.DMA((2,)),
            pltpu.SemaphoreType.DMA((n_copies,)),
            pltpu.SemaphoreType.DMA((n_copies,)),
        ],
        compiler_params=pltpu.CompilerParams(
            collective_id=0, has_side_effects=True, vmem_limit_bytes=48 * 2**20
        ),
        name="pair_grads",
    )(images, text_embed, log_scale, logit_bias)


def solution(mesh):
    in_specs = (P(("blk", "grp"), None), P(("blk", "grp"), None), P(), P())
    out_specs = (P(("blk", "grp"), None), P(("blk", "grp"), None))
    return jax.shard_map(
        per_device, mesh=mesh, in_specs=in_specs, out_specs=out_specs, check_vma=False
    )
```

```python
import jax
import jax.numpy as jnp
from jax import lax
from jax.experimental import pallas as pl
from jax.experimental.pallas import tpu as pltpu
from jax.sharding import PartitionSpec as P

EPS = 1e-06
R = 128
HALF = R // 2
NX, NZ, NBLK = 4, 8, 16

SEGMENTS = (
    ("a", 16, "-", "A"),
    ("b", 32, "-", "A"),
    ("e", 32, "-", "B"),
    ("c", 16, "+", "B"),
    ("d", 32, "+", "B"),
)
BATCHES = (
    (("O", "*"), ("P1", "*")),
    (("P2", "a"), ("P2", "b"), ("P2", "e"), ("Q", "c"), ("Q", "d")),
    (("P2", "c"), ("P2", "d"), ("Q", "a"), ("Q", "b"), ("Q", "e")),
)
PAIRS = {"A": (0, 0), "B": (1, 1), "C": (2, 3), "D": (3, 2)}
ORDER = (
    "f_a", "f_b", "f_e", "n_d", "n_c", "n_e", "r_lo", "l_hi", "r_hi", "l_lo", "t_0", "o_d",
    "o_c", "o_a", "r2", "l2", "n_b", "n_a", "t_3", "t_1", "o_b", "f_d", "t_2", "f_c", "o_e",
    "z1A", "z1D", "z1B", "z1C", "d1", "bof_d", "z0C", "z0D", "bfo_b", "z0B", "bof_c", "bfo_a",
    "z0A", "d0", "z2A", "z2D", "z2C", "z2B", "d2", "bof_e", "j1d", "bn_e", "bf_d", "igD", "igB",
    "c2", "igA", "j1a", "bon_a", "c0", "igC", "c3", "c1", "j1b", "bon_b", "j1c", "bf_c", "bn_c",
    "bn_d", "jx2", "x2l", "x2r", "j1e", "bf_e", "jx3l", "x3l", "jx1h", "x1h", "j2a", "bn_a",
    "jx3h", "x3h", "jx1l", "x1l", "j2b", "bn_b", "finI", "finT",
)


def layout():
    offset, at = {}, 0
    for name, count, _, _ in SEGMENTS:
        offset[name] = (at, count)
        at += count
    place, spans, at = {}, [], 0
    for pieces in BATCHES:
        start = at
        for block, name in pieces:
            if name == "*":
                for other, (low, count) in offset.items():
                    place[block, other] = (at + low, count)
                at += R
            else:
                place[block, name] = (at, offset[name][1])
                at += offset[name][1]
        spans.append((start, at - start))
    return offset, place, spans


def kernel(
    img_hbm, txt_hbm, ls_ref, lb_ref, oimg_ref, otxt_ref,
    raw_img, raw_txt, imgs, txts, w_ref, dt_f, dt_b, join_in, own_in, far_in,
    di_f, di_out, di_in, xs, xh_in, xf_in, in_sem, send_sem, recv_sem,
):
    blk = lax.axis_index("blk")
    grp = lax.axis_index("grp")
    core = lax.rem(grp, 2)
    x = lax.rem(grp // 2, NX)
    z = lax.rem(blk, 4) + 4 * (grp // 8)
    f32, bf = jnp.float32, jnp.bfloat16

    def at(dblk, dz, dx=0, dcore=0):
        new_z = lax.rem(z + dz, NZ)
        new_x = lax.rem(x + dx, NX)
        new_core = lax.rem(core + dcore, 2)
        return (lax.rem(blk + dblk, NBLK), (new_z // 4 * NX + new_x) * 2 + new_core)

    near, near_back = at(1, 1), at(15, 7)
    far, far_back = at(1, 5), at(15, 3)
    right, left, twin = at(0, 0, 1), at(0, 0, 3), at(0, 0, 0, 1)

    loads = [
        pltpu.make_async_copy(src, dst, in_sem.at[i])
        for i, (src, dst) in enumerate(((txt_hbm, raw_txt), (img_hbm, raw_img)))
    ]
    for load in loads:
        load.start()
    barrier = pltpu.get_barrier_semaphore()
    peers = (near, near_back, far, far_back, right, left, twin)
    for peer in peers:
        pl.semaphore_signal(barrier, inc=1, device_id=peer, device_id_type=pl.DeviceIdType.MESH)

    copies, waited = {}, set()

    def send(name, src, dst, to):
        k = len(copies)
        copies[name] = pltpu.make_async_remote_copy(
            src_ref=src, dst_ref=dst, send_sem=send_sem.at[k], recv_sem=recv_sem.at[k],
            device_id=to, device_id_type=pl.DeviceIdType.MESH,
        )
        copies[name].start()

    def arrived(*names):
        for name in names:
            if name not in waited:
                waited.add(name)
                copies[name].wait_recv()

    def rows(ref, span):
        return ref.at[pl.ds(*span)]

    def get(ref, span):
        return ref[span[0] : span[0] + span[1], :]

    def unitize(values):
        values = values.astype(f32)
        inverse = lax.rsqrt(jnp.sum(values * values, axis=-1, keepdims=True) + EPS)
        return values * inverse, inverse

    def project(raw, grad_hat):
        unit, inverse = unitize(raw)
        inner = jnp.sum(grad_hat * unit, axis=-1, keepdims=True)
        return inverse * (grad_hat - inner * unit)

    offset, place, spans = layout()
    steps = {}

    def step(name, needs, run, *args):
        steps[name] = (needs, run, args)

    def step_send(name, needs, *args):
        step(name, needs, send, name, *args)

    for k, _, way, _ in SEGMENTS:
        own, p1, p2, q = (place[block, k] for block in ("O", "P1", "P2", "Q"))
        step_send("n_" + k, (), rows(txts, own), rows(txts, p1), near)
        if way == "+":
            step_send("o_" + k, ("n_" + k,), rows(txts, p1), rows(txts, q), far_back)
            step_send("f_" + k, ("o_" + k,), rows(txts, q), rows(txts, p2), near)
        else:
            step_send("f_" + k, (), rows(txts, own), rows(txts, p2), far)
            step_send("o_" + k, ("f_" + k,), rows(txts, p2), rows(txts, q), near_back)

    def image(dx, part=None, other=0):
        base = next(q for q, d in PAIRS.values() if d == dx) * 2 * R + other * R
        return (base, R) if part is None else (base + part * HALF, HALF)

    def step_image(name, needs, src, dst, to):
        step_send(name, needs, rows(imgs, src), rows(imgs, dst), to)

    step_image("r_lo", (), image(0, 0), image(3, 0), right)
    step_image("l_hi", (), image(0, 1), image(1, 1), left)
    step_image("r_hi", (), image(0, 1), image(3, 1), right)
    step_image("l_lo", (), image(0, 0), image(1, 0), left)
    step_image("r2", ("r_lo",), image(3, 0), image(2, 0), right)
    step_image("l2", ("l_hi",), image(1, 1), image(2, 1), left)
    step_image("t_0", (), image(0), image(0, None, 1), twin)
    step_image("t_3", ("r_lo", "r_hi"), image(3), image(3, None, 1), twin)
    step_image("t_1", ("l_lo", "l_hi"), image(1), image(1, None, 1), twin)
    step_image("t_2", ("r2", "l2"), image(2), image(2, None, 1), twin)
    image_needs = {
        "A": ("t_0",), "B": ("l_lo", "l_hi", "t_1"), "C": ("r_lo", "r_hi", "t_3"), "D": ("r2", "l2", "t_2"),
    }

    def score(start, count, q, labelled):
        logits = lax.dot_general(
            txts[start : start + count, :], imgs[q * 256 : q * 256 + 256, :],
            (((1,), (1,)), ((), ())), preferred_element_type=f32,
        )
        weight = jax.nn.sigmoid(temper * logits + bias)
        if labelled:
            row = lax.broadcasted_iota(jnp.int32, (count, 256), 0)
            col = lax.broadcasted_iota(jnp.int32, (count, 256), 1)
            weight = weight - jnp.logical_and(row == col, row < R).astype(f32)
        w_ref[start : start + count, q * 256 : q * 256 + 256] = (temper * weight).astype(bf)

    def text_grads(start, count):
        grad = jnp.dot(w_ref[start : start + count, :], imgs[...], preferred_element_type=f32)
        dt_f[start : start + count, :] = grad
        dt_b[start : start + count, :] = grad.astype(bf)

    for b, (pieces, (start, count)) in enumerate(zip(BATCHES, spans)):
        needs = ()
        for block, name in pieces:
            if block != "O":
                prefix = {"P1": "n_", "P2": "f_", "Q": "o_"}[block]
                needs += tuple(prefix + k for k in (offset if name == "*" else (name,)))
        for letter, (q, _) in PAIRS.items():
            step("z%d%s" % (b, letter), needs + image_needs[letter], score, start, count, q, (b, q) == (0, 0))
        step("d%d" % b, (), text_grads, start, count)

    def join(span, slot):
        start, count = span
        total = dt_f[start : start + count, :] + get(join_in, slot).astype(f32)
        dt_b[start : start + count, :] = total.astype(bf)

    low = 0
    for k, count, _, way in SEGMENTS:
        own, p1, p2, q = (place[block, k] for block in ("O", "P1", "P2", "Q"))
        slot, slot2 = (low, count), (low + count, count)
        if way == "A":
            low += 2 * count
            step_send("bfo_" + k, (), rows(dt_b, p2), rows(join_in, slot), near_back)
            step("j1" + k, ("bfo_" + k,), join, q, slot)
            step_send("bon_" + k, (), rows(dt_b, q), rows(join_in, slot2), far)
            step("j2" + k, ("bon_" + k,), join, p1, slot2)
        else:
            low += count
            step_send("bof_" + k, (), rows(dt_b, q), rows(join_in, slot), near)
            step("j1" + k, ("bof_" + k,), join, p2, slot)
            step_send("bf_" + k, (), rows(dt_b, p2), rows(far_in, offset[k]), far_back)
        step_send("bn_" + k, (), rows(dt_b, p1), rows(own_in, offset[k]), near_back)

    def final_text():
        for k, _, _, way in SEGMENTS:
            own, here = place["O", k], offset[k]
            total = get(dt_f, own) + get(own_in, here).astype(f32)
            if way == "B":
                total = total + get(far_in, here).astype(f32)
            otxt_ref[here[0] : here[0] + here[1], :] = project(get(raw_txt, here), total)

    step("finT", tuple(("bn_" if way == "A" else "bf_") + k for k, _, _, way in SEGMENTS)
         + tuple("bn_" + k for k, _, _, way in SEGMENTS if way == "B"), final_text)

    def image_grads(q):
        grad = lax.dot_general(
            w_ref[:, q * 256 : q * 256 + 256], txts[...], (((0,), (0,)), ((), ())),
            preferred_element_type=f32,
        )
        di_f[q * R : q * R + R, :] = grad[0:R, :]
        di_out[q * R : q * R + R, :] = grad[R : 2 * R, :].astype(bf)

    block = {dx: q * R for q, dx in PAIRS.values()}

    def both(dx, part=None):
        span = (block[dx], R) if part is None else (block[dx] + part * HALF, HALF)
        return get(di_f, span) + get(di_in, span).astype(f32)

    for letter, (q, dx) in PAIRS.items():
        step("ig" + letter, (), image_grads, q)
        span = (block[dx], R)
        step_send("c%d" % dx, (), rows(di_out, span), rows(di_in, span), twin)

    def stage(dx, part, received=None):
        start = block[dx] + part * HALF
        total = both(dx, part)
        if received is not None:
            total = total + xh_in[received * HALF : received * HALF + HALF, :].astype(f32)
        xs[start : start + HALF, :] = total.astype(bf)

    def stage_two():
        stage(2, 0)
        stage(2, 1)

    def staged(dx, part):
        return rows(xs, (block[dx] + part * HALF, HALF))

    step("jx2", ("c2",), stage_two)
    step_send("x2r", (), staged(2, 0), rows(xh_in, (0, HALF)), right)
    step_send("x2l", (), staged(2, 1), rows(xh_in, (HALF, HALF)), left)
    step("jx1h", ("c1",), stage, 1, 1)
    step_send("x1h", (), staged(1, 1), rows(xf_in, (HALF, HALF)), right)
    step("jx3l", ("c3",), stage, 3, 0)
    step_send("x3l", (), staged(3, 0), rows(xf_in, (R, HALF)), left)
    step("jx1l", ("c1", "x2r"), stage, 1, 0, 0)
    step_send("x1l", (), staged(1, 0), rows(xf_in, (0, HALF)), right)
    step("jx3h", ("c3", "x2l"), stage, 3, 1, 1)
    step_send("x3h", (), staged(3, 1), rows(xf_in, (R + HALF, HALF)), left)

    def final_image():
        total = both(0) + get(xf_in, (0, R)).astype(f32) + get(xf_in, (R, R)).astype(f32)
        oimg_ref[...] = project(raw_img[...], total)

    step("finI", ("c0", "x1h", "x1l", "x3l", "x3h"), final_image)

    loads[0].wait()
    unit, _ = unitize(raw_txt[...])
    txts[0:R, :] = unit.astype(bf)
    loads[1].wait()
    unit, _ = unitize(raw_img[...])
    imgs[0:R, :] = unit.astype(bf)
    temper = jnp.exp(jnp.full((1, 256), ls_ref[0], f32))
    bias = jnp.full((1, 256), lb_ref[0], f32)
    pl.semaphore_wait(barrier, len(peers))

    for name in ORDER:
        needs, run, args = steps[name]
        arrived(*needs)
        run(*args)
    for copy in copies.values():
        copy.wait_send()


def per_device(images, text_embed, log_scale, logit_bias):
    d = images.shape[1]
    bf, f32 = jnp.bfloat16, jnp.float32
    vmem = pl.BlockSpec(memory_space=pltpu.VMEM)
    hbm = pl.BlockSpec(memory_space=pltpu.HBM)
    smem = pl.BlockSpec(memory_space=pltpu.SMEM)
    n_copies = 56
    return pl.pallas_call(
        kernel,
        out_shape=(jax.ShapeDtypeStruct((R, d), f32),) * 2,
        in_specs=[hbm, hbm, smem, smem],
        out_specs=(vmem, vmem),
        scratch_shapes=[
            pltpu.VMEM((R, d), bf),
            pltpu.VMEM((R, d), bf),
            pltpu.VMEM((8 * R, d), bf),
            pltpu.VMEM((4 * R, d), bf),
            pltpu.VMEM((4 * R, 8 * R), bf),
            pltpu.VMEM((4 * R, d), f32),
            pltpu.VMEM((4 * R, d), bf),
            pltpu.VMEM((2 * R, d), bf),
            pltpu.VMEM((R, d), bf),
            pltpu.VMEM((R, d), bf),
            pltpu.VMEM((4 * R, d), f32),
            pltpu.VMEM((4 * R, d), bf),
            pltpu.VMEM((4 * R, d), bf),
            pltpu.VMEM((4 * R, d), bf),
            pltpu.VMEM((R, d), bf),
            pltpu.VMEM((2 * R, d), bf),
            pltpu.SemaphoreType.DMA((2,)),
            pltpu.SemaphoreType.DMA((n_copies,)),
            pltpu.SemaphoreType.DMA((n_copies,)),
        ],
        compiler_params=pltpu.CompilerParams(
            collective_id=0, has_side_effects=True, vmem_limit_bytes=48 * 2**20
        ),
        name="pair_grads",
    )(images, text_embed, log_scale, logit_bias)


def solution(mesh):
    in_specs = (P(("blk", "grp"), None), P(("blk", "grp"), None), P(), P())
    out_specs = (P(("blk", "grp"), None), P(("blk", "grp"), None))
    return jax.shard_map(
        per_device, mesh=mesh, in_specs=in_specs, out_specs=out_specs, check_vma=False
    )
```

```python
import jax
import jax.numpy as jnp
from jax import lax
from jax.experimental import pallas as pl
from jax.experimental.pallas import tpu as pltpu
from jax.sharding import PartitionSpec as P

EPS = 1e-06
R = 128
HALF = R // 2
NX, NZ, NBLK = 4, 8, 16

SEGMENTS = (
    ("a", 16, "-", "A"),
    ("b", 32, "-", "A"),
    ("e", 16, "-", "B"),
    ("h", 16, "-", "B"),
    ("c", 16, "+", "B"),
    ("d", 32, "+", "B"),
)
BATCHES = (
    (("O", "*"), ("P1", "*")),
    (("P2", "a"), ("P2", "b"), ("P2", "e"), ("P2", "h"), ("Q", "c"), ("Q", "d")),
    (("P2", "c"), ("Q", "a"), ("Q", "b")),
    (("P2", "d"), ("Q", "e"), ("Q", "h")),
)
PAIRS = {"A": (0, 0), "B": (1, 1), "C": (2, 3), "D": (3, 2)}
ORDER = (
    "f_h", "n_d", "n_c", "n_h", "f_e", "n_b", "f_b", "r_lo", "l_hi", "t_0", "f_a", "r_hi",
    "l_lo", "o_d", "o_c", "o_h", "l2", "r2", "o_e", "t_3", "t_1", "n_a", "o_b", "t_2", "f_d",
    "o_a", "f_c", "z1B", "n_e", "z1A", "z1D", "z1C", "d1", "bof_c", "bof_d", "bfo_a", "z3C",
    "z3A", "z3B", "z3D", "bfo_b", "d3", "bof_h", "z2B", "z2D", "z2A", "z2C", "d2", "j1a",
    "bon_a", "j1c", "bf_c", "z0D", "igD", "c2", "z0C", "igC", "j1d", "bof_e", "c3", "bf_d",
    "j1b", "bon_b", "j1h", "z0B", "igB", "c1", "jx2", "x2l", "x2r", "z0A", "d0", "bn_h", "igA",
    "bn_e", "j2a", "c0", "jx3l", "j1e", "bf_e", "x3l", "bn_c", "bf_h", "jx1h", "x1h", "bn_d",
    "jx3h", "jx1l", "x1l", "x3h", "j2b", "bn_b", "bn_a", "finI", "finT",
)


def layout():
    offset, at = {}, 0
    for name, count, _, _ in SEGMENTS:
        offset[name] = (at, count)
        at += count
    place, spans, at = {}, [], 0
    for pieces in BATCHES:
        start = at
        for block, name in pieces:
            if name == "*":
                for other, (low, count) in offset.items():
                    place[block, other] = (at + low, count)
                at += R
            else:
                place[block, name] = (at, offset[name][1])
                at += offset[name][1]
        spans.append((start, at - start))
    return offset, place, spans


def kernel(
    raw, ls_ref, lb_ref, oimg_ref, otxt_ref,
    imgs, txts, w_ref, dt_f, dt_b, join_in, own_in, far_in,
    di_f, di_out, di_in, xs, xh_in, xf_in, send_sem, recv_sem,
):
    blk = lax.axis_index("blk")
    grp = lax.axis_index("grp")
    core = lax.rem(grp, 2)
    x = lax.rem(grp // 2, NX)
    z = lax.rem(blk, 4) + 4 * (grp // 8)
    f32, bf = jnp.float32, jnp.bfloat16

    def at(dblk, dz, dx=0, dcore=0):
        new_z = lax.rem(z + dz, NZ)
        new_x = lax.rem(x + dx, NX)
        new_core = lax.rem(core + dcore, 2)
        return (lax.rem(blk + dblk, NBLK), (new_z // 4 * NX + new_x) * 2 + new_core)

    near, near_back = at(1, 1), at(15, 7)
    far, far_back = at(1, 5), at(15, 3)
    right, left, twin = at(0, 0, 1), at(0, 0, 3), at(0, 0, 0, 1)

    barrier = pltpu.get_barrier_semaphore()
    peers = (near, near_back, far, far_back, right, left, twin)
    for peer in peers:
        pl.semaphore_signal(barrier, inc=1, device_id=peer, device_id_type=pl.DeviceIdType.MESH)

    copies, waited = {}, set()

    def send(name, src, dst, to):
        k = len(copies)
        copies[name] = pltpu.make_async_remote_copy(
            src_ref=src, dst_ref=dst, send_sem=send_sem.at[k], recv_sem=recv_sem.at[k],
            device_id=to, device_id_type=pl.DeviceIdType.MESH,
        )
        copies[name].start()

    def arrived(*names):
        for name in names:
            if name not in waited:
                waited.add(name)
                copies[name].wait_recv()

    def rows(ref, span):
        return ref.at[pl.ds(*span)]

    def get(ref, span):
        return ref[span[0] : span[0] + span[1], :]

    def unitize(values):
        values = values.astype(f32)
        inverse = lax.rsqrt(jnp.sum(values * values, axis=-1, keepdims=True) + EPS)
        return values * inverse, inverse

    def project(raw, grad_hat):
        unit, inverse = unitize(raw)
        inner = jnp.sum(grad_hat * unit, axis=-1, keepdims=True)
        return inverse * (grad_hat - inner * unit)

    offset, place, spans = layout()
    steps = {}

    def step(name, needs, run, *args):
        steps[name] = (needs, run, args)

    def step_send(name, needs, *args):
        step(name, needs, send, name, *args)

    for k, _, way, _ in SEGMENTS:
        own, p1, p2, q = (place[block, k] for block in ("O", "P1", "P2", "Q"))
        step_send("n_" + k, (), rows(txts, own), rows(txts, p1), near)
        if way == "+":
            step_send("o_" + k, ("n_" + k,), rows(txts, p1), rows(txts, q), far_back)
            step_send("f_" + k, ("o_" + k,), rows(txts, q), rows(txts, p2), near)
        else:
            step_send("f_" + k, (), rows(txts, own), rows(txts, p2), far)
            step_send("o_" + k, ("f_" + k,), rows(txts, p2), rows(txts, q), near_back)

    def image(dx, part=None, other=0):
        base = next(q for q, d in PAIRS.values() if d == dx) * 2 * R + other * R
        return (base, R) if part is None else (base + part * HALF, HALF)

    def step_image(name, needs, src, dst, to):
        step_send(name, needs, rows(imgs, src), rows(imgs, dst), to)

    step_image("r_lo", (), image(0, 0), image(3, 0), right)
    step_image("l_hi", (), image(0, 1), image(1, 1), left)
    step_image("r_hi", (), image(0, 1), image(3, 1), right)
    step_image("l_lo", (), image(0, 0), image(1, 0), left)
    step_image("r2", ("r_lo",), image(3, 0), image(2, 0), right)
    step_image("l2", ("l_hi",), image(1, 1), image(2, 1), left)
    step_image("t_0", (), image(0), image(0, None, 1), twin)
    step_image("t_3", ("r_lo", "r_hi"), image(3), image(3, None, 1), twin)
    step_image("t_1", ("l_lo", "l_hi"), image(1), image(1, None, 1), twin)
    step_image("t_2", ("r2", "l2"), image(2), image(2, None, 1), twin)
    image_needs = {
        "A": ("t_0",), "B": ("l_lo", "l_hi", "t_1"), "C": ("r_lo", "r_hi", "t_3"), "D": ("r2", "l2", "t_2"),
    }

    def score(start, count, q, labelled):
        logits = lax.dot_general(
            txts[start : start + count, :], imgs[q * 256 : q * 256 + 256, :],
            (((1,), (1,)), ((), ())), preferred_element_type=f32,
        )
        weight = jax.nn.sigmoid(temper * logits + bias)
        if labelled:
            row = lax.broadcasted_iota(jnp.int32, (count, 256), 0)
            col = lax.broadcasted_iota(jnp.int32, (count, 256), 1)
            weight = weight - jnp.logical_and(row == col, row < R).astype(f32)
        w_ref[start : start + count, q * 256 : q * 256 + 256] = (temper * weight).astype(bf)

    def text_grads(start, count):
        grad = jnp.dot(w_ref[start : start + count, :], imgs[...], preferred_element_type=f32)
        dt_f[start : start + count, :] = grad
        dt_b[start : start + count, :] = grad.astype(bf)

    for b, (pieces, (start, count)) in enumerate(zip(BATCHES, spans)):
        needs = ()
        for block, name in pieces:
            if block != "O":
                prefix = {"P1": "n_", "P2": "f_", "Q": "o_"}[block]
                needs += tuple(prefix + k for k in (offset if name == "*" else (name,)))
        for letter, (q, _) in PAIRS.items():
            step("z%d%s" % (b, letter), needs + image_needs[letter], score, start, count, q, (b, q) == (0, 0))
        step("d%d" % b, (), text_grads, start, count)

    def join(span, slot):
        start, count = span
        total = dt_f[start : start + count, :] + get(join_in, slot).astype(f32)
        dt_b[start : start + count, :] = total.astype(bf)

    low = 0
    for k, count, _, way in SEGMENTS:
        own, p1, p2, q = (place[block, k] for block in ("O", "P1", "P2", "Q"))
        slot, slot2 = (low, count), (low + count, count)
        if way == "A":
            low += 2 * count
            step_send("bfo_" + k, (), rows(dt_b, p2), rows(join_in, slot), near_back)
            step("j1" + k, ("bfo_" + k,), join, q, slot)
            step_send("bon_" + k, (), rows(dt_b, q), rows(join_in, slot2), far)
            step("j2" + k, ("bon_" + k,), join, p1, slot2)
        else:
            low += count
            step_send("bof_" + k, (), rows(dt_b, q), rows(join_in, slot), near)
            step("j1" + k, ("bof_" + k,), join, p2, slot)
            step_send("bf_" + k, (), rows(dt_b, p2), rows(far_in, offset[k]), far_back)
        step_send("bn_" + k, (), rows(dt_b, p1), rows(own_in, offset[k]), near_back)

    def final_text():
        for k, _, _, way in SEGMENTS:
            own, here = place["O", k], offset[k]
            total = get(dt_f, own) + get(own_in, here).astype(f32)
            if way == "B":
                total = total + get(far_in, here).astype(f32)
            otxt_ref[here[0] : here[0] + here[1], :] = project(get(raw, here), total)

    step("finT", tuple(("bn_" if way == "A" else "bf_") + k for k, _, _, way in SEGMENTS)
         + tuple("bn_" + k for k, _, _, way in SEGMENTS if way == "B"), final_text)

    def image_grads(q):
        grad = lax.dot_general(
            w_ref[:, q * 256 : q * 256 + 256], txts[...], (((0,), (0,)), ((), ())),
            preferred_element_type=f32,
        )
        di_f[q * R : q * R + R, :] = grad[0:R, :]
        di_out[q * R : q * R + R, :] = grad[R : 2 * R, :].astype(bf)

    block = {dx: q * R for q, dx in PAIRS.values()}

    def both(dx, part=None):
        span = (block[dx], R) if part is None else (block[dx] + part * HALF, HALF)
        return get(di_f, span) + get(di_in, span).astype(f32)

    for letter, (q, dx) in PAIRS.items():
        step("ig" + letter, (), image_grads, q)
        span = (block[dx], R)
        step_send("c%d" % dx, (), rows(di_out, span), rows(di_in, span), twin)

    def stage(dx, part, received=None):
        start = block[dx] + part * HALF
        total = both(dx, part)
        if received is not None:
            total = total + xh_in[received * HALF : received * HALF + HALF, :].astype(f32)
        xs[start : start + HALF, :] = total.astype(bf)

    def stage_two():
        stage(2, 0)
        stage(2, 1)

    def staged(dx, part):
        return rows(xs, (block[dx] + part * HALF, HALF))

    step("jx2", ("c2",), stage_two)
    step_send("x2r", (), staged(2, 0), rows(xh_in, (0, HALF)), right)
    step_send("x2l", (), staged(2, 1), rows(xh_in, (HALF, HALF)), left)
    step("jx1h", ("c1",), stage, 1, 1)
    step_send("x1h", (), staged(1, 1), rows(xf_in, (HALF, HALF)), right)
    step("jx3l", ("c3",), stage, 3, 0)
    step_send("x3l", (), staged(3, 0), rows(xf_in, (R, HALF)), left)
    step("jx1l", ("c1", "x2r"), stage, 1, 0, 0)
    step_send("x1l", (), staged(1, 0), rows(xf_in, (0, HALF)), right)
    step("jx3h", ("c3", "x2l"), stage, 3, 1, 1)
    step_send("x3h", (), staged(3, 1), rows(xf_in, (R + HALF, HALF)), left)

    def final_image():
        total = both(0) + get(xf_in, (0, R)).astype(f32) + get(xf_in, (R, R)).astype(f32)
        oimg_ref[...] = project(get(raw, (R, R)), total)

    step("finI", ("c0", "x1h", "x1l", "x3l", "x3h"), final_image)

    unit, _ = unitize(raw[0:R, :])
    txts[0:R, :] = unit.astype(bf)
    unit, _ = unitize(raw[R : 2 * R, :])
    imgs[0:R, :] = unit.astype(bf)
    temper = jnp.exp(jnp.broadcast_to(ls_ref[...], (1, 256)))
    bias = jnp.broadcast_to(lb_ref[...], (1, 256))
    pl.semaphore_wait(barrier, len(peers))

    for name in ORDER:
        needs, run, args = steps[name]
        arrived(*needs)
        run(*args)
    for copy in copies.values():
        copy.wait_send()


def per_device(images, text_embed, log_scale, logit_bias):
    d = images.shape[1]
    bf, f32 = jnp.bfloat16, jnp.float32
    vmem = pl.BlockSpec(memory_space=pltpu.VMEM)
    raw = jnp.concatenate([text_embed, images], axis=0)
    n_copies = 64
    return pl.pallas_call(
        kernel,
        out_shape=(jax.ShapeDtypeStruct((R, d), f32),) * 2,
        in_specs=[vmem, vmem, vmem],
        out_specs=(vmem, vmem),
        scratch_shapes=[
            pltpu.VMEM((8 * R, d), bf),
            pltpu.VMEM((4 * R, d), bf),
            pltpu.VMEM((4 * R, 8 * R), bf),
            pltpu.VMEM((4 * R, d), f32),
            pltpu.VMEM((4 * R, d), bf),
            pltpu.VMEM((2 * R, d), bf),
            pltpu.VMEM((R, d), bf),
            pltpu.VMEM((R, d), bf),
            pltpu.VMEM((4 * R, d), f32),
            pltpu.VMEM((4 * R, d), bf),
            pltpu.VMEM((4 * R, d), bf),
            pltpu.VMEM((4 * R, d), bf),
            pltpu.VMEM((R, d), bf),
            pltpu.VMEM((2 * R, d), bf),
            pltpu.SemaphoreType.DMA((n_copies,)),
            pltpu.SemaphoreType.DMA((n_copies,)),
        ],
        compiler_params=pltpu.CompilerParams(
            collective_id=0, has_side_effects=True, vmem_limit_bytes=48 * 2**20
        ),
        name="pair_grads",
    )(raw, log_scale.reshape(1, 1), logit_bias.reshape(1, 1))


def solution(mesh):
    in_specs = (P(("blk", "grp"), None), P(("blk", "grp"), None), P(), P())
    out_specs = (P(("blk", "grp"), None), P(("blk", "grp"), None))
    return jax.shard_map(
        per_device, mesh=mesh, in_specs=in_specs, out_specs=out_specs, check_vma=False
    )
```

```python
import jax
import jax.numpy as jnp
from jax import lax
from jax.experimental import pallas as pl
from jax.experimental.pallas import tpu as pltpu
from jax.sharding import PartitionSpec as P

EPS = 1e-06
R = 128
HALF = R // 2
NX, NZ, NBLK = 4, 8, 16

SEGMENTS = (
    ("a", 16, "-", "A"),
    ("b", 32, "-", "A"),
    ("e", 16, "-", "B"),
    ("h", 16, "-", "B"),
    ("c", 16, "+", "B"),
    ("d", 32, "+", "B"),
)
BATCHES = (
    (("O", "*"), ("P1", "*")),
    (("P2", "a"), ("P2", "b"), ("P2", "e"), ("P2", "h"), ("Q", "c"), ("Q", "d")),
    (("P2", "c"), ("P2", "d"), ("Q", "a"), ("Q", "b"), ("Q", "e"), ("Q", "h")),
)
PAIRS = {"A": (0, 0), "B": (1, 1), "C": (2, 3), "D": (3, 2)}
ORDER = (
    "n_c", "n_d", "f_e", "l_hi", "r_lo", "n_a", "f_a", "f_h", "l_lo", "t_0", "r_hi", "o_c",
    "o_d", "f_b", "l2", "r2", "n_h", "t_1", "n_e", "t_2", "n_b", "o_a", "o_e", "o_h", "t_3",
    "f_c", "f_d", "o_b", "z1D", "z1A", "z1B", "z1C", "d1", "bof_d", "bfo_b", "bof_c", "z0B",
    "z0C", "bfo_a", "z0D", "z2A", "z2D", "z2B", "z2C", "d2", "bof_e", "j1b", "bon_b", "j1d",
    "bf_d", "igD", "c2", "igB", "c1", "bof_h", "j1a", "igC", "z0A", "igA", "jx2", "x2r", "x2l",
    "bon_a", "c3", "j1e", "jx3l", "jx1h", "x1h", "x3l", "bf_e", "d0", "bn_h", "bn_c", "bn_e",
    "j1h", "j1c", "jx3h", "bf_h", "bn_d", "jx1l", "x1l", "j2a", "bf_c", "x3h", "bn_a", "j2b",
    "c0", "bn_b", "finI", "finT",
)


def layout():
    offset, at = {}, 0
    for name, count, _, _ in SEGMENTS:
        offset[name] = (at, count)
        at += count
    place, spans, at = {}, [], 0
    for pieces in BATCHES:
        start = at
        for block, name in pieces:
            if name == "*":
                for other, (low, count) in offset.items():
                    place[block, other] = (at + low, count)
                at += R
            else:
                place[block, name] = (at, offset[name][1])
                at += offset[name][1]
        spans.append((start, at - start))
    return offset, place, spans


def kernel(
    raw, ls_ref, lb_ref, oimg_ref, otxt_ref,
    imgs, txts, w_ref, dt_f, dt_b, join_in, own_in, far_in,
    di_f, di_out, di_in, xs, xh_in, xf_in, send_sem, recv_sem,
):
    blk = lax.axis_index("blk")
    grp = lax.axis_index("grp")
    core = lax.rem(grp, 2)
    x = lax.rem(grp // 2, NX)
    z = lax.rem(blk, 4) + 4 * (grp // 8)
    f32, bf = jnp.float32, jnp.bfloat16

    def at(dblk, dz, dx=0, dcore=0):
        new_z = lax.rem(z + dz, NZ)
        new_x = lax.rem(x + dx, NX)
        new_core = lax.rem(core + dcore, 2)
        return (lax.rem(blk + dblk, NBLK), (new_z // 4 * NX + new_x) * 2 + new_core)

    near, near_back = at(1, 1), at(15, 7)
    far, far_back = at(1, 5), at(15, 3)
    right, left, twin = at(0, 0, 1), at(0, 0, 3), at(0, 0, 0, 1)

    barrier = pltpu.get_barrier_semaphore()
    peers = (near, near_back, far, far_back, right, left, twin)
    for peer in peers:
        pl.semaphore_signal(barrier, inc=1, device_id=peer, device_id_type=pl.DeviceIdType.MESH)

    copies, waited = {}, set()

    def send(name, src, dst, to):
        k = len(copies)
        copies[name] = pltpu.make_async_remote_copy(
            src_ref=src, dst_ref=dst, send_sem=send_sem.at[k], recv_sem=recv_sem.at[k],
            device_id=to, device_id_type=pl.DeviceIdType.MESH,
        )
        copies[name].start()

    def arrived(*names):
        for name in names:
            if name not in waited:
                waited.add(name)
                copies[name].wait_recv()

    def rows(ref, span):
        return ref.at[pl.ds(*span)]

    def get(ref, span):
        return ref[span[0] : span[0] + span[1], :]

    def unitize(values):
        values = values.astype(f32)
        inverse = lax.rsqrt(jnp.sum(values * values, axis=-1, keepdims=True) + EPS)
        return values * inverse, inverse

    def project(raw, grad_hat):
        unit, inverse = unitize(raw)
        inner = jnp.sum(grad_hat * unit, axis=-1, keepdims=True)
        return inverse * (grad_hat - inner * unit)

    offset, place, spans = layout()
    steps = {}

    def step(name, needs, run, *args):
        steps[name] = (needs, run, args)

    def step_send(name, needs, *args):
        step(name, needs, send, name, *args)

    for k, _, way, _ in SEGMENTS:
        own, p1, p2, q = (place[block, k] for block in ("O", "P1", "P2", "Q"))
        step_send("n_" + k, (), rows(txts, own), rows(txts, p1), near)
        if way == "+":
            step_send("o_" + k, ("n_" + k,), rows(txts, p1), rows(txts, q), far_back)
            step_send("f_" + k, ("o_" + k,), rows(txts, q), rows(txts, p2), near)
        else:
            step_send("f_" + k, (), rows(txts, own), rows(txts, p2), far)
            step_send("o_" + k, ("f_" + k,), rows(txts, p2), rows(txts, q), near_back)

    def image(dx, part=None, other=0):
        base = next(q for q, d in PAIRS.values() if d == dx) * 2 * R + other * R
        return (base, R) if part is None else (base + part * HALF, HALF)

    def step_image(name, needs, src, dst, to):
        step_send(name, needs, rows(imgs, src), rows(imgs, dst), to)

    step_image("r_lo", (), image(0, 0), image(3, 0), right)
    step_image("l_hi", (), image(0, 1), image(1, 1), left)
    step_image("r_hi", (), image(0, 1), image(3, 1), right)
    step_image("l_lo", (), image(0, 0), image(1, 0), left)
    step_image("r2", ("r_lo",), image(3, 0), image(2, 0), right)
    step_image("l2", ("l_hi",), image(1, 1), image(2, 1), left)
    step_image("t_0", (), image(0), image(0, None, 1), twin)
    step_image("t_3", ("r_lo", "r_hi"), image(3), image(3, None, 1), twin)
    step_image("t_1", ("l_lo", "l_hi"), image(1), image(1, None, 1), twin)
    step_image("t_2", ("r2", "l2"), image(2), image(2, None, 1), twin)
    image_needs = {
        "A": ("t_0",), "B": ("l_lo", "l_hi", "t_1"), "C": ("r_lo", "r_hi", "t_3"), "D": ("r2", "l2", "t_2"),
    }

    def score(start, count, q, labelled):
        logits = lax.dot_general(
            txts[start : start + count, :], imgs[q * 256 : q * 256 + 256, :],
            (((1,), (1,)), ((), ())), preferred_element_type=f32,
        )
        weight = jax.nn.sigmoid(temper * logits + bias)
        if labelled:
            row = lax.broadcasted_iota(jnp.int32, (count, 256), 0)
            col = lax.broadcasted_iota(jnp.int32, (count, 256), 1)
            weight = weight - jnp.logical_and(row == col, row < R).astype(f32)
        w_ref[start : start + count, q * 256 : q * 256 + 256] = (temper * weight).astype(bf)

    def text_grads(start, count):
        grad = jnp.dot(w_ref[start : start + count, :], imgs[...], preferred_element_type=f32)
        dt_f[start : start + count, :] = grad
        dt_b[start : start + count, :] = grad.astype(bf)

    for b, (pieces, (start, count)) in enumerate(zip(BATCHES, spans)):
        needs = ()
        for block, name in pieces:
            if block != "O":
                prefix = {"P1": "n_", "P2": "f_", "Q": "o_"}[block]
                needs += tuple(prefix + k for k in (offset if name == "*" else (name,)))
        for letter, (q, _) in PAIRS.items():
            step("z%d%s" % (b, letter), needs + image_needs[letter], score, start, count, q, (b, q) == (0, 0))
        step("d%d" % b, (), text_grads, start, count)

    def join(span, slot):
        start, count = span
        total = dt_f[start : start + count, :] + get(join_in, slot).astype(f32)
        dt_b[start : start + count, :] = total.astype(bf)

    low = 0
    for k, count, _, way in SEGMENTS:
        own, p1, p2, q = (place[block, k] for block in ("O", "P1", "P2", "Q"))
        slot, slot2 = (low, count), (low + count, count)
        if way == "A":
            low += 2 * count
            step_send("bfo_" + k, (), rows(dt_b, p2), rows(join_in, slot), near_back)
            step("j1" + k, ("bfo_" + k,), join, q, slot)
            step_send("bon_" + k, (), rows(dt_b, q), rows(join_in, slot2), far)
            step("j2" + k, ("bon_" + k,), join, p1, slot2)
        else:
            low += count
            step_send("bof_" + k, (), rows(dt_b, q), rows(join_in, slot), near)
            step("j1" + k, ("bof_" + k,), join, p2, slot)
            step_send("bf_" + k, (), rows(dt_b, p2), rows(far_in, offset[k]), far_back)
        step_send("bn_" + k, (), rows(dt_b, p1), rows(own_in, offset[k]), near_back)

    def final_text():
        for k, _, _, way in SEGMENTS:
            own, here = place["O", k], offset[k]
            total = get(dt_f, own) + get(own_in, here).astype(f32)
            if way == "B":
                total = total + get(far_in, here).astype(f32)
            otxt_ref[here[0] : here[0] + here[1], :] = project(get(raw, here), total)

    step("finT", tuple(("bn_" if way == "A" else "bf_") + k for k, _, _, way in SEGMENTS)
         + tuple("bn_" + k for k, _, _, way in SEGMENTS if way == "B"), final_text)

    def image_grads(q):
        grad = lax.dot_general(
            w_ref[:, q * 256 : q * 256 + 256], txts[...], (((0,), (0,)), ((), ())),
            preferred_element_type=f32,
        )
        di_f[q * R : q * R + R, :] = grad[0:R, :]
        di_out[q * R : q * R + R, :] = grad[R : 2 * R, :].astype(bf)

    block = {dx: q * R for q, dx in PAIRS.values()}

    def both(dx, part=None):
        span = (block[dx], R) if part is None else (block[dx] + part * HALF, HALF)
        return get(di_f, span) + get(di_in, span).astype(f32)

    for letter, (q, dx) in PAIRS.items():
        step("ig" + letter, (), image_grads, q)
        span = (block[dx], R)
        step_send("c%d" % dx, (), rows(di_out, span), rows(di_in, span), twin)

    def stage(dx, part, received=None):
        start = block[dx] + part * HALF
        total = both(dx, part)
        if received is not None:
            total = total + xh_in[received * HALF : received * HALF + HALF, :].astype(f32)
        xs[start : start + HALF, :] = total.astype(bf)

    def stage_two():
        stage(2, 0)
        stage(2, 1)

    def staged(dx, part):
        return rows(xs, (block[dx] + part * HALF, HALF))

    step("jx2", ("c2",), stage_two)
    step_send("x2r", (), staged(2, 0), rows(xh_in, (0, HALF)), right)
    step_send("x2l", (), staged(2, 1), rows(xh_in, (HALF, HALF)), left)
    step("jx1h", ("c1",), stage, 1, 1)
    step_send("x1h", (), staged(1, 1), rows(xf_in, (HALF, HALF)), right)
    step("jx3l", ("c3",), stage, 3, 0)
    step_send("x3l", (), staged(3, 0), rows(xf_in, (R, HALF)), left)
    step("jx1l", ("c1", "x2r"), stage, 1, 0, 0)
    step_send("x1l", (), staged(1, 0), rows(xf_in, (0, HALF)), right)
    step("jx3h", ("c3", "x2l"), stage, 3, 1, 1)
    step_send("x3h", (), staged(3, 1), rows(xf_in, (R + HALF, HALF)), left)

    def final_image():
        total = both(0) + get(xf_in, (0, R)).astype(f32) + get(xf_in, (R, R)).astype(f32)
        oimg_ref[...] = project(get(raw, (R, R)), total)

    step("finI", ("c0", "x1h", "x1l", "x3l", "x3h"), final_image)

    unit, _ = unitize(raw[0:R, :])
    txts[0:R, :] = unit.astype(bf)
    unit, _ = unitize(raw[R : 2 * R, :])
    imgs[0:R, :] = unit.astype(bf)
    temper = jnp.exp(jnp.broadcast_to(ls_ref[...], (1, 256)))
    bias = jnp.broadcast_to(lb_ref[...], (1, 256))
    pl.semaphore_wait(barrier, len(peers))

    for name in ORDER:
        needs, run, args = steps[name]
        arrived(*needs)
        run(*args)
    for copy in copies.values():
        copy.wait_send()


def per_device(images, text_embed, log_scale, logit_bias):
    d = images.shape[1]
    bf, f32 = jnp.bfloat16, jnp.float32
    vmem = pl.BlockSpec(memory_space=pltpu.VMEM)
    raw = jnp.concatenate([text_embed, images], axis=0)
    n_copies = 64
    return pl.pallas_call(
        kernel,
        out_shape=(jax.ShapeDtypeStruct((R, d), f32),) * 2,
        in_specs=[vmem, vmem, vmem],
        out_specs=(vmem, vmem),
        scratch_shapes=[
            pltpu.VMEM((8 * R, d), bf),
            pltpu.VMEM((4 * R, d), bf),
            pltpu.VMEM((4 * R, 8 * R), bf),
            pltpu.VMEM((4 * R, d), f32),
            pltpu.VMEM((4 * R, d), bf),
            pltpu.VMEM((2 * R, d), bf),
            pltpu.VMEM((R, d), bf),
            pltpu.VMEM((R, d), bf),
            pltpu.VMEM((4 * R, d), f32),
            pltpu.VMEM((4 * R, d), bf),
            pltpu.VMEM((4 * R, d), bf),
            pltpu.VMEM((4 * R, d), bf),
            pltpu.VMEM((R, d), bf),
            pltpu.VMEM((2 * R, d), bf),
            pltpu.SemaphoreType.DMA((n_copies,)),
            pltpu.SemaphoreType.DMA((n_copies,)),
        ],
        compiler_params=pltpu.CompilerParams(
            collective_id=0, has_side_effects=True, vmem_limit_bytes=48 * 2**20
        ),
        name="pair_grads",
    )(raw, log_scale.reshape(1, 1), logit_bias.reshape(1, 1))


def solution(mesh):
    in_specs = (P(("blk", "grp"), None), P(("blk", "grp"), None), P(), P())
    out_specs = (P(("blk", "grp"), None), P(("blk", "grp"), None))
    return jax.shard_map(
        per_device, mesh=mesh, in_specs=in_specs, out_specs=out_specs, check_vma=False
    )
```

```python
import jax
import jax.numpy as jnp
from jax import lax
from jax.experimental import pallas as pl
from jax.experimental.pallas import tpu as pltpu
from jax.sharding import PartitionSpec as P

EPS = 1e-06
R = 128
HALF = R // 2
NX, NZ, NBLK = 4, 8, 16

SEGMENTS = (
    ("a", 16, "-", "A"),
    ("b", 32, "-", "A"),
    ("e", 16, "-", "B"),
    ("h", 16, "-", "B"),
    ("c", 16, "+", "B"),
    ("d", 32, "+", "B"),
)
BATCHES = (
    (("O", "*"), ("P1", "*")),
    (("P2", "a"), ("P2", "b"), ("P2", "e"), ("P2", "h"), ("Q", "c"), ("Q", "d")),
    (("P2", "c"), ("Q", "a"), ("Q", "b")),
    (("P2", "d"), ("Q", "e"), ("Q", "h")),
)
PAIRS = {"A": (0, 0), "B": (1, 1), "C": (2, 3), "D": (3, 2)}
ORDER = (
    "n_c", "f_a", "r_lo", "n_d", "f_h", "l_hi", "n_e", "r_hi", "t_0", "l_lo", "o_c", "f_b",
    "n_a", "o_d", "r2", "l2", "t_3", "n_h", "t_1", "f_e", "o_b", "n_b", "t_2", "o_a", "f_c",
    "o_h", "f_d", "z1B", "o_e", "z1D", "z1C", "z1A", "d1", "bfo_b", "bof_c", "z0D", "bof_d",
    "z2A", "z2C", "z0B", "bfo_a", "z2D", "z2B", "d2", "z3D", "igD", "c2", "z3B", "j1c", "bf_c",
    "z3C", "j1b", "bon_b", "z3A", "z0C", "d3", "bof_h", "igC", "j1a", "c3", "bon_a", "igB",
    "jx2", "x2r", "bof_e", "x2l", "c1", "j1d", "bf_d", "z0A", "igA", "jx3l", "x3l", "jx1h",
    "x1h", "d0", "bn_c", "bn_d", "c0", "j1e", "bf_e", "jx1l", "x1l", "bn_h", "jx3h", "x3h",
    "j2a", "bn_e", "j2b", "j1h", "bn_a", "bf_h", "bn_b", "finI", "finT",
)


def layout():
    offset, at = {}, 0
    for name, count, _, _ in SEGMENTS:
        offset[name] = (at, count)
        at += count
    place, spans, at = {}, [], 0
    for pieces in BATCHES:
        start = at
        for block, name in pieces:
            if name == "*":
                for other, (low, count) in offset.items():
                    place[block, other] = (at + low, count)
                at += R
            else:
                place[block, name] = (at, offset[name][1])
                at += offset[name][1]
        spans.append((start, at - start))
    return offset, place, spans


def kernel(
    raw, ls_ref, lb_ref, oimg_ref, otxt_ref,
    imgs, txts, w_ref, dt_f, dt_b, join_in, own_in, far_in,
    di_f, di_out, di_in, xs, xh_in, xf_in, send_sem, recv_sem,
):
    blk = lax.axis_index("blk")
    grp = lax.axis_index("grp")
    core = lax.rem(grp, 2)
    x = lax.rem(grp // 2, NX)
    z = lax.rem(blk, 4) + 4 * (grp // 8)
    f32, bf = jnp.float32, jnp.bfloat16

    def at(dblk, dz, dx=0, dcore=0):
        new_z = lax.rem(z + dz, NZ)
        new_x = lax.rem(x + dx, NX)
        new_core = lax.rem(core + dcore, 2)
        return (lax.rem(blk + dblk, NBLK), (new_z // 4 * NX + new_x) * 2 + new_core)

    near, near_back = at(1, 1), at(15, 7)
    far, far_back = at(1, 5), at(15, 3)
    right, left, twin = at(0, 0, 1), at(0, 0, 3), at(0, 0, 0, 1)

    barrier = pltpu.get_barrier_semaphore()
    peers = (near, near_back, far, far_back, right, left, twin)
    for peer in peers:
        pl.semaphore_signal(barrier, inc=1, device_id=peer, device_id_type=pl.DeviceIdType.MESH)

    copies, waited = {}, set()

    def send(name, src, dst, to):
        k = len(copies)
        copies[name] = pltpu.make_async_remote_copy(
            src_ref=src, dst_ref=dst, send_sem=send_sem.at[k], recv_sem=recv_sem.at[k],
            device_id=to, device_id_type=pl.DeviceIdType.MESH,
        )
        copies[name].start()

    def arrived(*names):
        for name in names:
            if name not in waited:
                waited.add(name)
                copies[name].wait_recv()

    def rows(ref, span):
        return ref.at[pl.ds(*span)]

    def get(ref, span):
        return ref[span[0] : span[0] + span[1], :]

    def unitize(values):
        values = values.astype(f32)
        inverse = lax.rsqrt(jnp.sum(values * values, axis=-1, keepdims=True) + EPS)
        return values * inverse, inverse

    def project(raw, grad_hat):
        unit, inverse = unitize(raw)
        inner = jnp.sum(grad_hat * unit, axis=-1, keepdims=True)
        return inverse * (grad_hat - inner * unit)

    offset, place, spans = layout()
    steps = {}

    def step(name, needs, run, *args):
        steps[name] = (needs, run, args)

    def step_send(name, needs, *args):
        step(name, needs, send, name, *args)

    for k, _, way, _ in SEGMENTS:
        own, p1, p2, q = (place[block, k] for block in ("O", "P1", "P2", "Q"))
        step_send("n_" + k, (), rows(txts, own), rows(txts, p1), near)
        if way == "+":
            step_send("o_" + k, ("n_" + k,), rows(txts, p1), rows(txts, q), far_back)
            step_send("f_" + k, ("o_" + k,), rows(txts, q), rows(txts, p2), near)
        else:
            step_send("f_" + k, (), rows(txts, own), rows(txts, p2), far)
            step_send("o_" + k, ("f_" + k,), rows(txts, p2), rows(txts, q), near_back)

    def image(dx, part=None, other=0):
        base = next(q for q, d in PAIRS.values() if d == dx) * 2 * R + other * R
        return (base, R) if part is None else (base + part * HALF, HALF)

    def step_image(name, needs, src, dst, to):
        step_send(name, needs, rows(imgs, src), rows(imgs, dst), to)

    step_image("r_lo", (), image(0, 0), image(3, 0), right)
    step_image("l_hi", (), image(0, 1), image(1, 1), left)
    step_image("r_hi", (), image(0, 1), image(3, 1), right)
    step_image("l_lo", (), image(0, 0), image(1, 0), left)
    step_image("r2", ("r_lo",), image(3, 0), image(2, 0), right)
    step_image("l2", ("l_hi",), image(1, 1), image(2, 1), left)
    step_image("t_0", (), image(0), image(0, None, 1), twin)
    step_image("t_3", ("r_lo", "r_hi"), image(3), image(3, None, 1), twin)
    step_image("t_1", ("l_lo", "l_hi"), image(1), image(1, None, 1), twin)
    step_image("t_2", ("r2", "l2"), image(2), image(2, None, 1), twin)
    image_needs = {
        "A": ("t_0",), "B": ("l_lo", "l_hi", "t_1"), "C": ("r_lo", "r_hi", "t_3"), "D": ("r2", "l2", "t_2"),
    }

    def score(start, count, q, labelled):
        logits = lax.dot_general(
            txts[start : start + count, :], imgs[q * 256 : q * 256 + 256, :],
            (((1,), (1,)), ((), ())), preferred_element_type=f32,
        )
        weight = jax.nn.sigmoid(temper * logits + bias)
        if labelled:
            row = lax.broadcasted_iota(jnp.int32, (count, 256), 0)
            col = lax.broadcasted_iota(jnp.int32, (count, 256), 1)
            weight = weight - jnp.logical_and(row == col, row < R).astype(f32)
        w_ref[start : start + count, q * 256 : q * 256 + 256] = (temper * weight).astype(bf)

    def text_grads(start, count):
        grad = jnp.dot(w_ref[start : start + count, :], imgs[...], preferred_element_type=f32)
        dt_f[start : start + count, :] = grad
        dt_b[start : start + count, :] = grad.astype(bf)

    for b, (pieces, (start, count)) in enumerate(zip(BATCHES, spans)):
        needs = ()
        for block, name in pieces:
            if block != "O":
                prefix = {"P1": "n_", "P2": "f_", "Q": "o_"}[block]
                needs += tuple(prefix + k for k in (offset if name == "*" else (name,)))
        for letter, (q, _) in PAIRS.items():
            step("z%d%s" % (b, letter), needs + image_needs[letter], score, start, count, q, (b, q) == (0, 0))
        step("d%d" % b, (), text_grads, start, count)

    def join(span, slot):
        start, count = span
        total = dt_f[start : start + count, :] + get(join_in, slot).astype(f32)
        dt_b[start : start + count, :] = total.astype(bf)

    low = 0
    for k, count, _, way in SEGMENTS:
        own, p1, p2, q = (place[block, k] for block in ("O", "P1", "P2", "Q"))
        slot, slot2 = (low, count), (low + count, count)
        if way == "A":
            low += 2 * count
            step_send("bfo_" + k, (), rows(dt_b, p2), rows(join_in, slot), near_back)
            step("j1" + k, ("bfo_" + k,), join, q, slot)
            step_send("bon_" + k, (), rows(dt_b, q), rows(join_in, slot2), far)
            step("j2" + k, ("bon_" + k,), join, p1, slot2)
        else:
            low += count
            step_send("bof_" + k, (), rows(dt_b, q), rows(join_in, slot), near)
            step("j1" + k, ("bof_" + k,), join, p2, slot)
            step_send("bf_" + k, (), rows(dt_b, p2), rows(far_in, offset[k]), far_back)
        step_send("bn_" + k, (), rows(dt_b, p1), rows(own_in, offset[k]), near_back)

    def final_text():
        for k, _, _, way in SEGMENTS:
            own, here = place["O", k], offset[k]
            total = get(dt_f, own) + get(own_in, here).astype(f32)
            if way == "B":
                total = total + get(far_in, here).astype(f32)
            otxt_ref[here[0] : here[0] + here[1], :] = project(get(raw, here), total)

    step("finT", tuple(("bn_" if way == "A" else "bf_") + k for k, _, _, way in SEGMENTS)
         + tuple("bn_" + k for k, _, _, way in SEGMENTS if way == "B"), final_text)

    def image_grads(q):
        grad = lax.dot_general(
            w_ref[:, q * 256 : q * 256 + 256], txts[...], (((0,), (0,)), ((), ())),
            preferred_element_type=f32,
        )
        di_f[q * R : q * R + R, :] = grad[0:R, :]
        di_out[q * R : q * R + R, :] = grad[R : 2 * R, :].astype(bf)

    block = {dx: q * R for q, dx in PAIRS.values()}

    def both(dx, part=None):
        span = (block[dx], R) if part is None else (block[dx] + part * HALF, HALF)
        return get(di_f, span) + get(di_in, span).astype(f32)

    for letter, (q, dx) in PAIRS.items():
        step("ig" + letter, (), image_grads, q)
        span = (block[dx], R)
        step_send("c%d" % dx, (), rows(di_out, span), rows(di_in, span), twin)

    def stage(dx, part, received=None):
        start = block[dx] + part * HALF
        total = both(dx, part)
        if received is not None:
            total = total + xh_in[received * HALF : received * HALF + HALF, :].astype(f32)
        xs[start : start + HALF, :] = total.astype(bf)

    def stage_two():
        stage(2, 0)
        stage(2, 1)

    def staged(dx, part):
        return rows(xs, (block[dx] + part * HALF, HALF))

    step("jx2", ("c2",), stage_two)
    step_send("x2r", (), staged(2, 0), rows(xh_in, (0, HALF)), right)
    step_send("x2l", (), staged(2, 1), rows(xh_in, (HALF, HALF)), left)
    step("jx1h", ("c1",), stage, 1, 1)
    step_send("x1h", (), staged(1, 1), rows(xf_in, (HALF, HALF)), right)
    step("jx3l", ("c3",), stage, 3, 0)
    step_send("x3l", (), staged(3, 0), rows(xf_in, (R, HALF)), left)
    step("jx1l", ("c1", "x2r"), stage, 1, 0, 0)
    step_send("x1l", (), staged(1, 0), rows(xf_in, (0, HALF)), right)
    step("jx3h", ("c3", "x2l"), stage, 3, 1, 1)
    step_send("x3h", (), staged(3, 1), rows(xf_in, (R + HALF, HALF)), left)

    def final_image():
        total = both(0) + get(xf_in, (0, R)).astype(f32) + get(xf_in, (R, R)).astype(f32)
        oimg_ref[...] = project(get(raw, (R, R)), total)

    step("finI", ("c0", "x1h", "x1l", "x3l", "x3h"), final_image)

    unit, _ = unitize(raw[0:R, :])
    txts[0:R, :] = unit.astype(bf)
    unit, _ = unitize(raw[R : 2 * R, :])
    imgs[0:R, :] = unit.astype(bf)
    temper = jnp.exp(jnp.broadcast_to(ls_ref[...], (1, 256)))
    bias = jnp.broadcast_to(lb_ref[...], (1, 256))
    pl.semaphore_wait(barrier, len(peers))

    for name in ORDER:
        needs, run, args = steps[name]
        arrived(*needs)
        run(*args)
    for copy in copies.values():
        copy.wait_send()


def per_device(images, text_embed, log_scale, logit_bias):
    d = images.shape[1]
    bf, f32 = jnp.bfloat16, jnp.float32
    vmem = pl.BlockSpec(memory_space=pltpu.VMEM)
    raw = jnp.concatenate([text_embed, images], axis=0)
    n_copies = 64
    return pl.pallas_call(
        kernel,
        out_shape=(jax.ShapeDtypeStruct((R, d), f32),) * 2,
        in_specs=[vmem, vmem, vmem],
        out_specs=(vmem, vmem),
        scratch_shapes=[
            pltpu.VMEM((8 * R, d), bf),
            pltpu.VMEM((4 * R, d), bf),
            pltpu.VMEM((4 * R, 8 * R), bf),
            pltpu.VMEM((4 * R, d), f32),
            pltpu.VMEM((4 * R, d), bf),
            pltpu.VMEM((2 * R, d), bf),
            pltpu.VMEM((R, d), bf),
            pltpu.VMEM((R, d), bf),
            pltpu.VMEM((4 * R, d), f32),
            pltpu.VMEM((4 * R, d), bf),
            pltpu.VMEM((4 * R, d), bf),
            pltpu.VMEM((4 * R, d), bf),
            pltpu.VMEM((R, d), bf),
            pltpu.VMEM((2 * R, d), bf),
            pltpu.SemaphoreType.DMA((n_copies,)),
            pltpu.SemaphoreType.DMA((n_copies,)),
        ],
        compiler_params=pltpu.CompilerParams(
            collective_id=0, has_side_effects=True, vmem_limit_bytes=48 * 2**20
        ),
        name="pair_grads",
    )(raw, log_scale.reshape(1, 1), logit_bias.reshape(1, 1))


def solution(mesh):
    in_specs = (P(("blk", "grp"), None), P(("blk", "grp"), None), P(), P())
    out_specs = (P(("blk", "grp"), None), P(("blk", "grp"), None))
    return jax.shard_map(
        per_device, mesh=mesh, in_specs=in_specs, out_specs=out_specs, check_vma=False
    )
```
